32 devices in a mesh: ctx: 16 (over z, x, core), head: 2 (over y).
Axes of the slice: x: 2, y: 2, z: 4, core: 2. Of those that a mesh axis runs over, the one named last changes fastest.
Arguments:
- queries: bfloat16 [16384, 4096], P('ctx', 'head')
- keys: bfloat16 [16384, 4096], P('ctx', 'head'), may hold values from -5 to 5
- values: bfloat16 [16384, 4096], P('ctx', 'head')
- log_decay: float32 [16384, 32], P('ctx', 'head'), as said below
- gate: bfloat16 [16384, 4096], P('ctx', 'head'), may hold values from -6 to 6
- norm_gain: float32 [4096], replicated, may hold values from 0.1 to 1.9
Outputs:
- output: bfloat16 [16384, 4096], P(('ctx', 'head'))
The draws below stay inside these ranges and needn't reach their ends.
Inputs may be any that keep to these rules, and one draw needn't show every extreme that they name: `log_decay`: every entry is at most 0.
All inputs are finite; a program needn't handle non-finite values.
Results may differ from the reference program's by a relative error of at most 0.0085.
Values may be sent and summed in bfloat16 or wider, within the bound.
A program may use at most 128 MiB of HBM per device.

```python
import math
import jax
import jax.numpy as jnp
from jax import lax

H = 32
HD = 128
TOK_DEV = 1024
HW = 4096
TOKENS = 16384


def draw_queries(key, part):
    first, second = jax.random.split(key)
    base = jnp.clip(jax.random.normal(first, (TOKENS, H, HD), jnp.float32), -4.0, 4.0)
    rows = jnp.exp(jax.random.uniform(second, (TOKENS, H, 1), jnp.float32, 0.0, math.log(10.0)))
    scaled = base * rows * (1.0 / math.sqrt(HD))
    return scaled.reshape(TOKENS, H * HD).astype(jnp.bfloat16)


def draw_values(key, part):
    column = jnp.arange(H * HD) // HD
    level = column.astype(jnp.float32) / (H - 1)
    base = jnp.clip(jax.random.normal(key, (TOKENS, H * HD), jnp.float32), -4.0, 4.0)
    scale = jnp.exp(level * math.log(10.0))
    return (base * scale[None, :]).astype(jnp.bfloat16)


def draw_log_decay(key, part):
    keys = jax.random.split(key, 7)
    order = jax.random.permutation(keys[0], H)
    fast_count = H // 2
    fast = order < fast_count
    slow_rate = jnp.exp(jax.random.uniform(keys[1], (H,), jnp.float32, math.log(0.03), math.log(0.3))) / TOKENS
    fast_rate = jnp.exp(jax.random.uniform(keys[2], (H,), jnp.float32, math.log(1.0 / 50.0), math.log(1.0 / 30.0)))
    forgetting_speed = jnp.where(fast, fast_rate, slow_rate)
    blocks = TOKENS // TOK_DEV
    segment_scaling_factor = jnp.exp(jax.random.uniform(keys[3], (blocks, 1, H), jnp.float32, -math.log(2.0), math.log(2.0)))
    segment_scaling_factor = jnp.broadcast_to(segment_scaling_factor, (blocks, TOK_DEV, H)).reshape(TOKENS, H)
    approximate_guess = jnp.exp(jax.random.uniform(keys[4], (TOKENS, H), jnp.float32, -0.33, 0.33))
    sample_indices = jax.random.randint(keys[5], (2, H), 0, TOKENS)
    objective_entries = jax.random.uniform(keys[6], (2, H), jnp.float32, math.log(0.5), math.log(0.8))
    target_index = jnp.arange(TOKENS)
    segment_partition = jnp.where(target_index[:, None] == sample_indices[0][None, :], objective_entries[0][None, :], 0.0)
    segment_partition = segment_partition + jnp.where(target_index[:, None] == sample_indices[1][None, :], objective_entries[1][None, :], 0.0)
    return (segment_partition - forgetting_speed[None, :] * segment_scaling_factor * approximate_guess).astype(jnp.float32)


def shard_levels(stream_key, shape, cuts, least, top_value):
    loudness, own = 1.0, jax.random.fold_in(stream_key, 6)
    for axis_at, blocks in cuts:
        steps = jnp.exp(jax.random.uniform(jax.random.fold_in(own, axis_at), (blocks,), jnp.float32, least / len(cuts), top_value / len(cuts)))
        loudness = loudness * jnp.repeat(steps, shape[axis_at] // blocks).reshape([-1 if axis == axis_at else 1 for axis in range(len(shape))])
    return loudness


def noise(rng, shape, width, limit, shards=(), held_as=jnp.bfloat16):
    values = jax.random.normal(rng, shape, jnp.float32) * width
    if len(shards) > 0:
        values = shard_levels(rng, shape, shards, -0.22, 0.18) * values
    return jnp.clip(values, min=-limit, max=limit).astype(held_as)


def setup_inputs(seed: int = 0) -> dict:
    seeds = jax.random.split(jax.random.key(seed), 7)
    queries = draw_queries(jax.random.fold_in(seeds[6], 71), 0)
    keys = noise(seeds[1], (TOKENS, HW), 1.0, 5.0, ((0, 16), (1, 2)))
    values = draw_values(jax.random.fold_in(seeds[6], 71), 0)
    log_decay = draw_log_decay(jax.random.fold_in(seeds[6], 71), 0)
    gate = noise(seeds[4], (TOKENS, HW), 1.5, 6.0, ((0, 16), (1, 2)))
    norm_gain = jnp.clip(1.0 + 0.18 * jax.random.normal(seeds[5], (HW,), jnp.float32), 0.1, 1.9)
    return dict(queries=queries, keys=keys, values=values, log_decay=log_decay, gate=gate, norm_gain=norm_gain)


eps_norm = 1e-05

def head_block(qh, kh, vh, ch):
    count = qh.shape[0]
    target_index = jnp.arange(count)
    causal = target_index[:, None] >= target_index[None, :]
    scores = jnp.dot(qh, kh.T, preferred_element_type=jnp.float32)
    spread = jnp.where(causal, ch[:, None] - ch[None, :], 0.0)
    weights = (scores * jnp.where(causal, jnp.exp(spread), 0.0)).astype(jnp.bfloat16)
    inner = jnp.dot(weights, vh, preferred_element_type=jnp.float32)
    keyed = kh.astype(jnp.float32) * jnp.exp(ch[-1] - ch)[:, None]
    state = jnp.dot(keyed.T, vh.astype(jnp.float32), precision=lax.Precision.HIGHEST)
    return (inner, state)

def split_heads(block, heads):
    count = block.shape[0]
    return block.reshape(count, heads, block.shape[1] // heads).transpose(1, 0, 2)

def local_block(queries, keys, values, log_decay):
    heads = log_decay.shape[1]
    cum = jnp.cumsum(log_decay, axis=0)
    inner, state = lax.map(lambda parts: head_block(parts[0], parts[1], parts[2], parts[3]), (split_heads(queries, heads), split_heads(keys, heads), split_heads(values, heads), cum.T))
    return (cum, inner, state)

def join_block(queries, cum, inner, carried):
    heads = cum.shape[1]
    count = queries.shape[0]
    qfloat = split_heads(queries, heads).astype(jnp.float32)
    across = jnp.einsum('hcd,hde->hce', qfloat, carried, precision=lax.Precision.HIGHEST)
    total = inner + jnp.exp(cum).T[:, :, None] * across
    return total.transpose(1, 0, 2).reshape(count, queries.shape[1]).astype(jnp.bfloat16)

def normalize(attended, gate, gain):
    shade = attended.astype(jnp.float32)
    scale = lax.rsqrt(lax.optimization_barrier(jnp.mean(shade * shade, axis=1, keepdims=True)) + eps_norm)
    return (shade * scale * gain * jax.nn.sigmoid(gate.astype(jnp.float32))).astype(jnp.bfloat16)

def reference(queries, keys, values, log_decay, gate, norm_gain):
    blocks = TOKENS // TOK_DEV

    def reshaped(array):
        return array.reshape(blocks, TOK_DEV, array.shape[1])

    def advance(carried, pieces):
        qblock, kblock, vblock, dblock = pieces
        cum, inner, state = local_block(qblock, kblock, vblock, dblock)
        attended = join_block(qblock, cum, inner, carried)
        carried = jnp.exp(cum[-1])[:, None, None] * carried + state
        return (carried, attended)
    start_state = jnp.zeros((H, HD, HD), jnp.float32)
    final_state, attended = lax.scan(advance, start_state, (reshaped(queries), reshaped(keys), reshaped(values), reshaped(log_decay)))
    attended = attended.reshape(TOKENS, H * HD)
    return normalize(attended, gate, norm_gain)
```

```python
import functools

import jax
import jax.numpy as jnp
from jax import lax
from jax.experimental import pallas as pl
from jax.experimental.pallas import tpu as pltpu
from jax.sharding import PartitionSpec as P

eps_norm = 1e-05
HD = 128
SUB = 256
f32 = jnp.float32
bf16 = jnp.bfloat16
MESH = pl.DeviceIdType.MESH


def dot(a, b, dims, precision=None):
    return lax.dot_general(a, b, (dims, ((), ())), precision=precision, preferred_element_type=f32)


def kernel(
    n_ctx, n_head, group, heads, ahead, fetch,
    q_hbm, k_hbm, v_hbm, g_hbm, ld_ref, gain_ref,
    out_hbm, ssq_ref,
    q_v, k_v, v_v, g_v, u_v, clt, clc, dlast, sst, mine, gath, tsend, tgath, ein, eout, acc, rows_own, rows_in,
    load_sem, gs_sem, gr_sem, ts_sem, tr_sem, es_sem, er_sem, ys_sem, yr_sem, own_sem, ss_sem, sr_sem,
):
    count = ld_ref.shape[1]
    subs = count // SUB
    rows = count // n_head
    planes = n_ctx // group
    ci = lax.axis_index("ctx")
    hi = lax.axis_index("head")
    plane = ci // group
    r = lax.rem(ci, group)
    base = plane * group
    first = plane == 0
    last = plane == planes - 1

    def peer(off):
        return base + lax.rem(r + off, group)

    def hpeer(off):
        return lax.rem(hi + off, n_head)

    barrier = pltpu.get_barrier_semaphore()

    def greet(**where):
        pl.semaphore_signal(barrier, inc=1, device_id=where, device_id_type=MESH)

    for off in range(1, group):
        greet(ctx=peer(off))
    for off in range(1, n_head):
        greet(head=hpeer(off))

    @pl.when(jnp.logical_not(first))
    def _():
        greet(ctx=ci - group)

    @pl.when(jnp.logical_not(last))
    def _():
        greet(ctx=ci + group)

    def cols(h):
        return pl.ds(pl.multiple_of(h * HD, HD), HD)

    def load(h, which):
        src, dst = ((k_hbm, k_v), (v_hbm, v_v), (q_hbm, q_v), (g_hbm, g_v))[which]
        return pltpu.make_async_copy(src.at[:, cols(h)], dst.at[:, cols(h)], load_sem.at[which, h])

    for h in range(fetch):
        load(h, 0).start()
        load(h, 1).start()
    for h in range(fetch):
        load(h, 2).start()
        load(h, 3).start()

    up = (
        lax.broadcasted_iota(jnp.int32, (SUB, SUB), 0) <= lax.broadcasted_iota(jnp.int32, (SUB, SUB), 1)
    ).astype(f32)
    total = jnp.zeros((heads, 1), f32)
    tall = []
    for s in range(subs):
        cl = dot(ld_ref[:, s * SUB:(s + 1) * SUB], up, ((1,), (0,)), lax.Precision.HIGHEST)
        clt[:, s * SUB:(s + 1) * SUB] = cl
        tall.append(jnp.transpose(cl))
        end = cl[:, SUB - 1:SUB]
        dlast[s] = jnp.broadcast_to(end, (heads, HD))
        total = total + end
    tsend[...] = jnp.broadcast_to(total, (heads, HD))
    acc[...] = jnp.zeros_like(acc)

    def tcopy(off):
        return pltpu.make_async_remote_copy(
            src_ref=tsend, dst_ref=tgath.at[r], send_sem=ts_sem.at[off], recv_sem=tr_sem.at[r],
            device_id={"ctx": peer(off)}, device_id_type=MESH)

    def gcopy(h, off):
        return pltpu.make_async_remote_copy(
            src_ref=mine.at[h], dst_ref=gath.at[r, h], send_sem=gs_sem.at[h, off], recv_sem=gr_sem.at[h, r],
            device_id={"ctx": peer(off)}, device_id_type=MESH)

    def grecv(h, slot):
        return pltpu.make_async_remote_copy(
            src_ref=mine.at[h], dst_ref=gath.at[slot, h], send_sem=gs_sem.at[h, 0], recv_sem=gr_sem.at[h, slot],
            device_id={"ctx": slot + base}, device_id_type=MESH)

    def trecv(slot):
        return pltpu.make_async_remote_copy(
            src_ref=tsend, dst_ref=tgath.at[slot], send_sem=ts_sem.at[0], recv_sem=tr_sem.at[slot],
            device_id={"ctx": slot + base}, device_id_type=MESH)

    def ecopy(h):
        return pltpu.make_async_remote_copy(
            src_ref=eout.at[h], dst_ref=ein.at[h], send_sem=es_sem.at[h], recv_sem=er_sem.at[h],
            device_id={"ctx": ci + group}, device_id_type=MESH)

    def place(j, h):
        return pl.ds(pl.multiple_of((j * heads + h) * HD, HD), HD)

    def ycopy(h, off):
        to = hpeer(off)
        part = pl.ds(pl.multiple_of(to * rows, rows), rows)
        return pltpu.make_async_remote_copy(
            src_ref=u_v.at[part, cols(h)], dst_ref=out_hbm.at[:, place(hi, h)],
            send_sem=ys_sem.at[h, off], recv_sem=yr_sem.at[h, hi],
            device_id={"head": to}, device_id_type=MESH)

    def yrecv(h, j):
        return pltpu.make_async_remote_copy(
            src_ref=u_v.at[pl.ds(0, rows), cols(h)], dst_ref=out_hbm.at[:, place(j, h)],
            send_sem=ys_sem.at[h, 0], recv_sem=yr_sem.at[h, j],
            device_id={"head": j}, device_id_type=MESH)

    def owncopy(h):
        part = pl.ds(pl.multiple_of(hi * rows, rows), rows)
        return pltpu.make_async_copy(u_v.at[part, cols(h)], out_hbm.at[:, place(hi, h)], own_sem.at[h])

    def scopy(off):
        to = hpeer(off)
        return pltpu.make_async_remote_copy(
            src_ref=rows_own.at[to], dst_ref=rows_in.at[hi], send_sem=ss_sem.at[off], recv_sem=sr_sem.at[hi],
            device_id={"head": to}, device_id_type=MESH)

    def srecv(j):
        return pltpu.make_async_remote_copy(
            src_ref=rows_own.at[j], dst_ref=rows_in.at[j], send_sem=ss_sem.at[0], recv_sem=sr_sem.at[j],
            device_id={"head": j}, device_id_type=MESH)

    def states(h):
        load(h, 0).wait()
        load(h, 1).wait()
        state = None
        for s in range(subs):
            span = slice(s * SUB, (s + 1) * SUB)
            col = clc[h, span, :]
            end = dlast[s, pl.ds(h, 1), :]
            keyed = (k_v[span, cols(h)].astype(f32) * jnp.exp(end - col)).astype(bf16)
            new = dot(keyed, v_v[span, cols(h)], ((0,), (0,)))
            sst[h, s] = new
            state = new if state is None else jnp.exp(end) * state + new
        mine[h] = state.astype(bf16)

    def spread_columns(h):
        for s in range(subs):
            span = slice(s * SUB, (s + 1) * SUB)
            clc[h, span, :] = jnp.broadcast_to(tall[s][:, h:h + 1], (SUB, HD))

    def share(h):
        for off in range(1, group):
            gcopy(h, off).start()

    def arrive(h):
        for slot in range(group):
            @pl.when(slot != r)
            def _():
                grecv(h, slot).wait_recv()

    def combine(h):
        arrive(h)
        own = mine[h].astype(f32)
        state = jnp.zeros((HD, HD), f32)
        within = state
        drop = jnp.zeros((1, HD), f32)
        before = drop
        for slot in range(group):
            here = slot == r
            within = jnp.where(here, state, within)
            before = jnp.where(here, drop, before)
            tot = jnp.where(here, tsend[pl.ds(h, 1), :], tgath[slot, pl.ds(h, 1), :])
            part = jnp.where(here, own, gath[slot, h].astype(f32))
            state = jnp.exp(tot) * state + part
            drop = drop + tot

        @pl.when(jnp.logical_not(first))
        def _():
            pltpu.make_async_remote_copy(
                src_ref=eout.at[h], dst_ref=ein.at[h], send_sem=es_sem.at[h], recv_sem=er_sem.at[h],
                device_id={"ctx": ci - group}, device_id_type=MESH).wait_recv()

        enter = jnp.where(first, 0.0, ein[h].astype(f32))
        eout[h] = (jnp.exp(drop) * enter + state).astype(bf16)

        @pl.when(jnp.logical_not(last))
        def _():
            ecopy(h).start()

        return within + jnp.exp(before) * enter

    causal = (
        lax.broadcasted_iota(jnp.int32, (SUB, SUB), 0) >= lax.broadcasted_iota(jnp.int32, (SUB, SUB), 1)
    )

    def attend(h, state):
        load(h, 2).wait()
        load(h, 3).wait()
        gain = gain_ref[pl.ds(hi * heads + h, 1), :]
        for s in range(subs):
            span = slice(s * SUB, (s + 1) * SUB)
            qs = q_v[span, cols(h)]
            col = clc[h, span, :]
            wide = jnp.concatenate([col] * (SUB // HD), axis=1)
            spread = jnp.where(causal, wide - clt[pl.ds(h, 1), span], -1e30)
            scores = dot(qs, k_v[span, cols(h)], ((1,), (1,)))
            weights = (scores * jnp.exp(spread)).astype(bf16)
            inner = dot(weights, v_v[span, cols(h)], ((1,), (0,)))
            across = dot(qs, state.astype(bf16), ((1,), (0,)))
            shade = (inner + jnp.exp(col) * across).astype(bf16).astype(f32)
            acc[span, :] += shade * shade
            gate = g_v[span, cols(h)].astype(f32)
            u_v[span, cols(h)] = (shade * gain * jax.nn.sigmoid(gate)).astype(bf16)
            if s < subs - 1:
                state = jnp.exp(dlast[s, pl.ds(h, 1), :]) * state + sst[h, s]

    spread_columns(0)
    states(0)
    waits = (group - 1) + (n_head - 1) + jnp.where(first, 0, 1) + jnp.where(last, 0, 1)
    pl.semaphore_wait(barrier, waits)
    for off in range(1, group):
        tcopy(off).start()
    share(0)

    def fetch_more(h, _):
        for which in range(4):
            load(h, which).start()
        return 0

    lax.fori_loop(fetch, heads, fetch_more, 0)
    for h in range(1, ahead):
        spread_columns(h)
        states(h)
        share(h)
    for h in range(ahead, heads):
        spread_columns(h)
    for slot in range(group):
        @pl.when(slot != r)
        def _():
            trecv(slot).wait_recv()

    def emit(h):
        state = combine(h)
        attend(h, state)
        for off in range(1, n_head):
            ycopy(h, off).start()
        owncopy(h).start()

    def step(h, _):
        emit(h)
        states(h + ahead)
        share(h + ahead)
        return 0

    def rest(h, _):
        emit(h)
        return 0

    lax.fori_loop(0, heads - ahead, step, 0)
    lax.fori_loop(heads - ahead, heads, rest, 0)

    ones = jnp.ones((8, HD), f32)
    for j in range(n_head):
        rows_own[j] = dot(ones, acc[j * rows:(j + 1) * rows, :], ((1,), (1,)), lax.Precision.HIGHEST)
    for off in range(1, n_head):
        scopy(off).start()

    def finish(h, _):
        for off in range(1, group):
            gcopy(h, off).wait_send()

        @pl.when(jnp.logical_not(last))
        def _():
            ecopy(h).wait_send()

        for off in range(1, n_head):
            ycopy(h, off).wait_send()
        owncopy(h).wait()
        for j in range(n_head):
            @pl.when(j != hi)
            def _():
                yrecv(h, j).wait_recv()
        return 0

    lax.fori_loop(0, heads, finish, 0)
    for off in range(1, group):
        tcopy(off).wait_send()
    for off in range(1, n_head):
        scopy(off).wait_send()
    for j in range(n_head):
        @pl.when(j != hi)
        def _():
            srecv(j).wait_recv()
    total = rows_own[hi]
    for j in range(n_head):
        total = total + jnp.where(j == hi, 0.0, rows_in[j])
    ssq_ref[...] = total


def body(n_ctx, n_head, queries, keys, values, log_decay, gate, norm_gain):
    count, heads = log_decay.shape
    width = queries.shape[1]
    columns = width * n_head
    rows = count // n_head
    group = 4 if n_ctx % 4 == 0 else 1
    subs = count // SUB
    gain = norm_gain.reshape(n_head * heads, HD)
    dma = pltpu.SemaphoreType.DMA
    whole = lambda dtype: pltpu.VMEM((count, width), dtype)
    anywhere = pl.BlockSpec(memory_space=pl.ANY)
    vmem = pl.BlockSpec(memory_space=pltpu.VMEM)
    out, ssq = pl.pallas_call(
        functools.partial(kernel, n_ctx, n_head, group, heads, min(2, heads), min(4, heads)),
        out_shape=(
            jax.ShapeDtypeStruct((rows, columns), bf16),
            jax.ShapeDtypeStruct((8, rows), f32),
        ),
        in_specs=[anywhere] * 4 + [vmem] * 2,
        out_specs=(anywhere, vmem),
        scratch_shapes=[
            whole(bf16), whole(bf16), whole(bf16), whole(bf16), whole(bf16),
            pltpu.VMEM((heads, count), f32),
            pltpu.VMEM((heads, count, HD), f32),
            pltpu.VMEM((subs, heads, HD), f32),
            pltpu.VMEM((heads, subs, HD, HD), f32),
            pltpu.VMEM((heads, HD, HD), bf16),
            pltpu.VMEM((group, heads, HD, HD), bf16),
            pltpu.VMEM((heads, HD), f32),
            pltpu.VMEM((group, heads, HD), f32),
            pltpu.VMEM((heads, HD, HD), bf16),
            pltpu.VMEM((heads, HD, HD), bf16),
            pltpu.VMEM((count, HD), f32),
            pltpu.VMEM((n_head, 8, rows), f32),
            pltpu.VMEM((n_head, 8, rows), f32),
            dma((4, heads)),
            dma((heads, group)), dma((heads, group)),
            dma((group,)), dma((group,)),
            dma((heads,)), dma((heads,)),
            dma((heads, n_head)), dma((heads, n_head)),
            dma((heads,)),
            dma((n_head,)), dma((n_head,)),
        ],
        compiler_params=pltpu.CompilerParams(
            collective_id=0, has_side_effects=True, vmem_limit_bytes=56 * 1024 * 1024
        ),
        cost_estimate=pl.CostEstimate(
            flops=heads * count * HD * (4 * SUB + 4 * HD),
            bytes_accessed=5 * count * width * 2,
            transcendentals=heads * count * (SUB + 3 * HD),
        ),
    )(queries, keys, values, gate, log_decay.T, gain)
    scale = lax.rsqrt(ssq[0] / columns + eps_norm)[:, None]
    return (out.astype(f32) * scale).astype(bf16)


def solution(mesh):
    spec = P("ctx", "head")
    return jax.shard_map(
        functools.partial(body, mesh.shape["ctx"], mesh.shape["head"]),
        mesh=mesh,
        in_specs=(spec, spec, spec, spec, spec, P()),
        out_specs=P(("ctx", "head"), None),
        check_vma=False,
    )
```

```python
import functools

import jax
import jax.numpy as jnp
from jax import lax
from jax.experimental import pallas as pl
from jax.experimental.pallas import tpu as pltpu
from jax.sharding import PartitionSpec as P

eps_norm = 1e-05
HD = 128
SUB = 256
f32 = jnp.float32
bf16 = jnp.bfloat16
MESH = pl.DeviceIdType.MESH


def dot(a, b, dims, precision=None):
    return lax.dot_general(a, b, (dims, ((), ())), precision=precision, preferred_element_type=f32)


def kernel(
    n_ctx, n_head, group, heads, ahead, fetch,
    q_hbm, k_hbm, v_hbm, g_hbm, ld_ref, gain_ref,
    out_hbm, ssq_ref,
    q_v, k_v, v_v, g_v, u_v, clt, clc, dlast, sst, mine, gath, tsend, tgath, ein, eout, acc, rows_own, rows_in,
    load_sem, gs_sem, gr_sem, ts_sem, tr_sem, es_sem, er_sem, ys_sem, yr_sem, own_sem, ss_sem, sr_sem,
):
    count = ld_ref.shape[1]
    subs = count // SUB
    rows = count // n_head
    planes = n_ctx // group
    ci = lax.axis_index("ctx")
    hi = lax.axis_index("head")
    plane = ci // group
    r = lax.rem(ci, group)
    base = plane * group
    first = plane == 0
    last = plane == planes - 1

    def peer(off):
        return base + lax.rem(r + off, group)

    def hpeer(off):
        return lax.rem(hi + off, n_head)

    barrier = pltpu.get_barrier_semaphore()

    def greet(**where):
        pl.semaphore_signal(barrier, inc=1, device_id=where, device_id_type=MESH)

    for off in range(1, group):
        greet(ctx=peer(off))
    for off in range(1, n_head):
        greet(head=hpeer(off))

    @pl.when(jnp.logical_not(first))
    def _():
        greet(ctx=ci - group)

    @pl.when(jnp.logical_not(last))
    def _():
        greet(ctx=ci + group)

    def cols(h):
        return pl.ds(pl.multiple_of(h * HD, HD), HD)

    def load(h, which):
        src, dst = ((k_hbm, k_v), (v_hbm, v_v), (q_hbm, q_v), (g_hbm, g_v))[which]
        return pltpu.make_async_copy(src.at[:, cols(h)], dst.at[:, cols(h)], load_sem.at[which, h])

    for h in range(fetch):
        for which in range(4):
            load(h, which).start()

    up = (
        lax.broadcasted_iota(jnp.int32, (SUB, SUB), 0) <= lax.broadcasted_iota(jnp.int32, (SUB, SUB), 1)
    ).astype(f32)
    total = jnp.zeros((heads, 1), f32)
    for s in range(subs):
        cl = dot(ld_ref[:, s * SUB:(s + 1) * SUB], up, ((1,), (0,)), lax.Precision.HIGHEST)
        clt[:, s * SUB:(s + 1) * SUB] = cl
        end = cl[:, SUB - 1:SUB]
        dlast[s] = jnp.broadcast_to(end, (heads, HD))
        total = total + end
    tsend[...] = jnp.broadcast_to(total, (heads, HD))
    acc[...] = jnp.zeros_like(acc)

    def tcopy(off):
        return pltpu.make_async_remote_copy(
            src_ref=tsend, dst_ref=tgath.at[r], send_sem=ts_sem.at[off], recv_sem=tr_sem.at[r],
            device_id={"ctx": peer(off)}, device_id_type=MESH)

    def gcopy(h, off):
        return pltpu.make_async_remote_copy(
            src_ref=mine.at[h], dst_ref=gath.at[r, h], send_sem=gs_sem.at[h, off], recv_sem=gr_sem.at[h, r],
            device_id={"ctx": peer(off)}, device_id_type=MESH)

    def grecv(h, slot):
        return pltpu.make_async_remote_copy(
            src_ref=mine.at[h], dst_ref=gath.at[slot, h], send_sem=gs_sem.at[h, 0], recv_sem=gr_sem.at[h, slot],
            device_id={"ctx": slot + base}, device_id_type=MESH)

    def trecv(slot):
        return pltpu.make_async_remote_copy(
            src_ref=tsend, dst_ref=tgath.at[slot], send_sem=ts_sem.at[0], recv_sem=tr_sem.at[slot],
            device_id={"ctx": slot + base}, device_id_type=MESH)

    def ecopy(h):
        return pltpu.make_async_remote_copy(
            src_ref=eout.at[h], dst_ref=ein.at[h], send_sem=es_sem.at[h], recv_sem=er_sem.at[h],
            device_id={"ctx": ci + group}, device_id_type=MESH)

    def place(j, h):
        return j * heads + h

    def ycopy(h, off):
        to = hpeer(off)
        part = pl.ds(pl.multiple_of(to * rows, rows), rows)
        return pltpu.make_async_remote_copy(
            src_ref=u_v.at[h, part], dst_ref=out_hbm.at[place(hi, h)],
            send_sem=ys_sem.at[h, off], recv_sem=yr_sem.at[h, hi],
            device_id={"head": to}, device_id_type=MESH)

    def yrecv(h, j):
        return pltpu.make_async_remote_copy(
            src_ref=u_v.at[h, pl.ds(0, rows)], dst_ref=out_hbm.at[place(j, h)],
            send_sem=ys_sem.at[h, 0], recv_sem=yr_sem.at[h, j],
            device_id={"head": j}, device_id_type=MESH)

    def owncopy(h):
        part = pl.ds(pl.multiple_of(hi * rows, rows), rows)
        return pltpu.make_async_copy(u_v.at[h, part], out_hbm.at[place(hi, h)], own_sem.at[h])

    def scopy(off):
        to = hpeer(off)
        return pltpu.make_async_remote_copy(
            src_ref=rows_own.at[to], dst_ref=rows_in.at[hi], send_sem=ss_sem.at[off], recv_sem=sr_sem.at[hi],
            device_id={"head": to}, device_id_type=MESH)

    def srecv(j):
        return pltpu.make_async_remote_copy(
            src_ref=rows_own.at[j], dst_ref=rows_in.at[j], send_sem=ss_sem.at[0], recv_sem=sr_sem.at[j],
            device_id={"head": j}, device_id_type=MESH)

    def states(h):
        load(h, 0).wait()
        load(h, 1).wait()
        state = None
        for s in range(subs):
            span = slice(s * SUB, (s + 1) * SUB)
            row = clt[pl.ds(h, 1), span]
            col = jnp.transpose(jnp.broadcast_to(row, (HD, SUB)))
            clc[h, span, :] = col
            end = dlast[s, pl.ds(h, 1), :]
            keyed = (k_v[span, cols(h)].astype(f32) * jnp.exp(end - col)).astype(bf16)
            new = dot(keyed, v_v[span, cols(h)], ((0,), (0,)))
            sst[h, s] = new
            state = new if state is None else jnp.exp(end) * state + new
        mine[h] = state.astype(bf16)

    def share(h):
        for off in range(1, group):
            gcopy(h, off).start()

    def arrive(h):
        for slot in range(group):
            @pl.when(slot != r)
            def _():
                grecv(h, slot).wait_recv()

    def combine(h):
        arrive(h)
        own = mine[h].astype(f32)
        state = jnp.zeros((HD, HD), f32)
        within = state
        drop = jnp.zeros((1, HD), f32)
        before = drop
        for slot in range(group):
            here = slot == r
            within = jnp.where(here, state, within)
            before = jnp.where(here, drop, before)
            tot = jnp.where(here, tsend[pl.ds(h, 1), :], tgath[slot, pl.ds(h, 1), :])
            part = jnp.where(here, own, gath[slot, h].astype(f32))
            state = jnp.exp(tot) * state + part
            drop = drop + tot

        @pl.when(jnp.logical_not(first))
        def _():
            pltpu.make_async_remote_copy(
                src_ref=eout.at[h], dst_ref=ein.at[h], send_sem=es_sem.at[h], recv_sem=er_sem.at[h],
                device_id={"ctx": ci - group}, device_id_type=MESH).wait_recv()

        enter = jnp.where(first, 0.0, ein[h].astype(f32))
        eout[h] = (jnp.exp(drop) * enter + state).astype(bf16)

        @pl.when(jnp.logical_not(last))
        def _():
            ecopy(h).start()

        return within + jnp.exp(before) * enter

    causal = (
        lax.broadcasted_iota(jnp.int32, (SUB, SUB), 0) >= lax.broadcasted_iota(jnp.int32, (SUB, SUB), 1)
    )

    def attend(h, state):
        load(h, 2).wait()
        load(h, 3).wait()
        gain = gain_ref[pl.ds(hi * heads + h, 1), :]
        for s in range(subs):
            span = slice(s * SUB, (s + 1) * SUB)
            qs = q_v[span, cols(h)]
            col = clc[h, span, :]
            wide = jnp.concatenate([col] * (SUB // HD), axis=1)
            spread = jnp.where(causal, wide - clt[pl.ds(h, 1), span], -1e30)
            scores = dot(qs, k_v[span, cols(h)], ((1,), (1,)))
            weights = (scores * jnp.exp(spread)).astype(bf16)
            inner = dot(weights, v_v[span, cols(h)], ((1,), (0,)))
            across = dot(qs, state.astype(bf16), ((1,), (0,)))
            shade = (inner + jnp.exp(col) * across).astype(bf16).astype(f32)
            acc[span, :] += shade * shade
            gate = g_v[span, cols(h)].astype(f32)
            opened = 0.5 * jnp.tanh(0.5 * gate) + 0.5
            u_v[h, span, :] = (shade * gain * opened).astype(bf16)
            if s < subs - 1:
                state = jnp.exp(dlast[s, pl.ds(h, 1), :]) * state + sst[h, s]

    states(0)
    waits = (group - 1) + (n_head - 1) + jnp.where(first, 0, 1) + jnp.where(last, 0, 1)
    pl.semaphore_wait(barrier, waits)
    for off in range(1, group):
        tcopy(off).start()
    share(0)

    for h in range(1, ahead):
        states(h)
        share(h)
    for slot in range(group):
        @pl.when(slot != r)
        def _():
            trecv(slot).wait_recv()

    def emit(h):
        state = combine(h)
        attend(h, state)
        for off in range(1, n_head):
            ycopy(h, off).start()
        owncopy(h).start()

    def step(h, _):
        for which in range(4):
            load(h + fetch, which).start()
        emit(h)
        states(h + ahead)
        share(h + ahead)
        return 0

    def later(h, _):
        emit(h)
        states(h + ahead)
        share(h + ahead)
        return 0

    def rest(h, _):
        emit(h)
        return 0

    lax.fori_loop(0, heads - fetch, step, 0)
    lax.fori_loop(heads - fetch, heads - ahead, later, 0)
    lax.fori_loop(heads - ahead, heads, rest, 0)

    ones = jnp.ones((8, HD), f32)
    for j in range(n_head):
        rows_own[j] = dot(ones, acc[j * rows:(j + 1) * rows, :], ((1,), (1,)), lax.Precision.HIGHEST)
    for off in range(1, n_head):
        scopy(off).start()

    def finish(h, _):
        for off in range(1, group):
            gcopy(h, off).wait_send()

        @pl.when(jnp.logical_not(last))
        def _():
            ecopy(h).wait_send()

        for off in range(1, n_head):
            ycopy(h, off).wait_send()
        owncopy(h).wait()
        for j in range(n_head):
            @pl.when(j != hi)
            def _():
                yrecv(h, j).wait_recv()
        return 0

    lax.fori_loop(0, heads, finish, 0)
    for off in range(1, group):
        tcopy(off).wait_send()
    for off in range(1, n_head):
        scopy(off).wait_send()
    for j in range(n_head):
        @pl.when(j != hi)
        def _():
            srecv(j).wait_recv()
    total = rows_own[hi]
    for j in range(n_head):
        total = total + jnp.where(j == hi, 0.0, rows_in[j])
    ssq_ref[...] = total


def rescale(columns, u_ref, ssq_ref, o_ref):
    block = o_ref.shape[0]
    row = lax.rsqrt(ssq_ref[0:1, :] / columns + eps_norm)
    scale = jnp.transpose(jnp.broadcast_to(row, (HD, block)))
    for h in range(u_ref.shape[0]):
        o_ref[:, h * HD:(h + 1) * HD] = (u_ref[h].astype(f32) * scale).astype(bf16)


def body(n_ctx, n_head, queries, keys, values, log_decay, gate, norm_gain):
    count, heads = log_decay.shape
    width = queries.shape[1]
    columns = width * n_head
    rows = count // n_head
    group = 4 if n_ctx % 4 == 0 else 1
    subs = count // SUB
    gain = norm_gain.reshape(n_head * heads, HD)
    dma = pltpu.SemaphoreType.DMA
    whole = lambda dtype: pltpu.VMEM((count, width), dtype)
    anywhere = pl.BlockSpec(memory_space=pl.ANY)
    vmem = pl.BlockSpec(memory_space=pltpu.VMEM)
    out, ssq = pl.pallas_call(
        functools.partial(kernel, n_ctx, n_head, group, heads, min(2, heads), min(3, heads)),
        out_shape=(
            jax.ShapeDtypeStruct((n_head * heads, rows, HD), bf16),
            jax.ShapeDtypeStruct((8, rows), f32),
        ),
        in_specs=[anywhere] * 4 + [vmem] * 2,
        out_specs=(anywhere, vmem),
        scratch_shapes=[
            whole(bf16), whole(bf16), whole(bf16), whole(bf16),
            pltpu.VMEM((heads, count, HD), bf16),
            pltpu.VMEM((heads, count), f32),
            pltpu.VMEM((heads, count, HD), f32),
            pltpu.VMEM((subs, heads, HD), f32),
            pltpu.VMEM((heads, subs, HD, HD), f32),
            pltpu.VMEM((heads, HD, HD), bf16),
            pltpu.VMEM((group, heads, HD, HD), bf16),
            pltpu.VMEM((heads, HD), f32),
            pltpu.VMEM((group, heads, HD), f32),
            pltpu.VMEM((heads, HD, HD), bf16),
            pltpu.VMEM((heads, HD, HD), bf16),
            pltpu.VMEM((count, HD), f32),
            pltpu.VMEM((n_head, 8, rows), f32),
            pltpu.VMEM((n_head, 8, rows), f32),
            dma((4, heads)),
            dma((heads, group)), dma((heads, group)),
            dma((group,)), dma((group,)),
            dma((heads,)), dma((heads,)),
            dma((heads, n_head)), dma((heads, n_head)),
            dma((heads,)),
            dma((n_head,)), dma((n_head,)),
        ],
        compiler_params=pltpu.CompilerParams(
            collective_id=0, has_side_effects=True, vmem_limit_bytes=46 * 1024 * 1024
        ),
        cost_estimate=pl.CostEstimate(
            flops=heads * count * HD * (4 * SUB + 4 * HD),
            bytes_accessed=5 * count * width * 2,
            transcendentals=heads * count * (SUB + 3 * HD),
        ),
    )(queries, keys, values, gate, log_decay.T, gain)
    block = min(128, rows)
    total_heads = n_head * heads
    return pl.pallas_call(
        functools.partial(rescale, columns),
        grid=(rows // block,),
        out_shape=jax.ShapeDtypeStruct((rows, columns), bf16),
        in_specs=[
            pl.BlockSpec((total_heads, block, HD), lambda i: (0, i, 0)),
            pl.BlockSpec((8, block), lambda i: (0, i)),
        ],
        out_specs=pl.BlockSpec((block, columns), lambda i: (i, 0)),
        compiler_params=pltpu.CompilerParams(vmem_limit_bytes=16 * 1024 * 1024),
        cost_estimate=pl.CostEstimate(
            flops=rows * columns, bytes_accessed=4 * rows * columns, transcendentals=rows),
    )(out, ssq)


def solution(mesh):
    spec = P("ctx", "head")
    return jax.shard_map(
        functools.partial(body, mesh.shape["ctx"], mesh.shape["head"]),
        mesh=mesh,
        in_specs=(spec, spec, spec, spec, spec, P()),
        out_specs=P(("ctx", "head"), None),
        check_vma=False,
    )
```

```python
import functools

import jax
import jax.numpy as jnp
from jax import lax
from jax.experimental import pallas as pl
from jax.experimental.pallas import tpu as pltpu
from jax.sharding import PartitionSpec as P

eps_norm = 1e-05
HD = 128
SUB = 256
f32 = jnp.float32
bf16 = jnp.bfloat16
MESH = pl.DeviceIdType.MESH


def dot(a, b, dims, precision=None):
    return lax.dot_general(a, b, (dims, ((), ())), precision=precision, preferred_element_type=f32)


def kernel(
    n_ctx, n_head, group, heads, ahead, fetch,
    q_hbm, k_hbm, v_hbm, g_hbm, ld_ref,
    out_hbm, scale_ref,
    inn, q_v, k_v, v_v, g_v, u_v, clt, clc, dlast, sst, mine, gath, tsend, tgath, ein, eout, acc, rows_own, rows_in,
    load_sem, gs_sem, gr_sem, ts_sem, tr_sem, es_sem, er_sem, ys_sem, yr_sem, own_sem, ss_sem, sr_sem,
):
    count = ld_ref.shape[1]
    columns = n_head * heads * HD
    subs = count // SUB
    rows = count // n_head
    planes = n_ctx // group
    ci = lax.axis_index("ctx")
    hi = lax.axis_index("head")
    plane = ci // group
    r = lax.rem(ci, group)
    base = plane * group
    first = plane == 0
    last = plane == planes - 1

    def peer(off):
        return base + lax.rem(r + off, group)

    def hpeer(off):
        return lax.rem(hi + off, n_head)

    barrier = pltpu.get_barrier_semaphore()

    def greet(**where):
        pl.semaphore_signal(barrier, inc=1, device_id=where, device_id_type=MESH)

    for off in range(1, group):
        greet(ctx=peer(off))
    for off in range(1, n_head):
        greet(head=hpeer(off))

    @pl.when(jnp.logical_not(first))
    def _():
        greet(ctx=ci - group)

    @pl.when(jnp.logical_not(last))
    def _():
        greet(ctx=ci + group)

    def cols(h):
        return pl.ds(pl.multiple_of(h * HD, HD), HD)

    def load(h, which):
        src, dst = ((k_hbm, k_v), (v_hbm, v_v), (q_hbm, q_v), (g_hbm, g_v))[which]
        return pltpu.make_async_copy(src.at[:, cols(h)], dst.at[:, cols(h)], load_sem.at[which, h])

    for h in range(fetch):
        for which in range(4):
            load(h, which).start()
    acc[...] = jnp.zeros_like(acc)

    up = (
        lax.broadcasted_iota(jnp.int32, (SUB, SUB), 0) <= lax.broadcasted_iota(jnp.int32, (SUB, SUB), 1)
    ).astype(f32).astype(bf16)
    parts = []
    for s in range(subs):
        left = ld_ref[:, s * SUB:(s + 1) * SUB]
        for _ in range(3):
            part = left.astype(bf16).astype(f32)
            parts.append(part)
            left = left - part
    sums = dot(jnp.concatenate(parts, axis=0).astype(bf16), up, ((1,), (0,)))
    total = jnp.zeros((heads, 1), f32)
    for s in range(subs):
        at = 3 * s * heads
        cl = (sums[at + 2 * heads:at + 3 * heads] + sums[at + heads:at + 2 * heads]) + sums[at:at + heads]
        clt[:, s * SUB:(s + 1) * SUB] = cl
        end = cl[:, SUB - 1:SUB]
        dlast[s] = jnp.broadcast_to(end, (heads, HD))
        total = total + end
    tsend[...] = jnp.broadcast_to(total, (heads, HD))

    def tcopy(off):
        return pltpu.make_async_remote_copy(
            src_ref=tsend, dst_ref=tgath.at[r], send_sem=ts_sem.at[off], recv_sem=tr_sem.at[r],
            device_id={"ctx": peer(off)}, device_id_type=MESH)

    def gcopy(h, off):
        return pltpu.make_async_remote_copy(
            src_ref=mine.at[h], dst_ref=gath.at[r, h], send_sem=gs_sem.at[h, off], recv_sem=gr_sem.at[h, r],
            device_id={"ctx": peer(off)}, device_id_type=MESH)

    def grecv(h, slot):
        return pltpu.make_async_remote_copy(
            src_ref=mine.at[h], dst_ref=gath.at[slot, h], send_sem=gs_sem.at[h, 0], recv_sem=gr_sem.at[h, slot],
            device_id={"ctx": slot + base}, device_id_type=MESH)

    def trecv(slot):
        return pltpu.make_async_remote_copy(
            src_ref=tsend, dst_ref=tgath.at[slot], send_sem=ts_sem.at[0], recv_sem=tr_sem.at[slot],
            device_id={"ctx": slot + base}, device_id_type=MESH)

    def ecopy(h):
        return pltpu.make_async_remote_copy(
            src_ref=eout.at[h], dst_ref=ein.at[h], send_sem=es_sem.at[h], recv_sem=er_sem.at[h],
            device_id={"ctx": ci + group}, device_id_type=MESH)

    def place(j, h):
        return j * heads + h

    def ycopy(h, off):
        to = hpeer(off)
        part = pl.ds(pl.multiple_of(to * rows, rows), rows)
        return pltpu.make_async_remote_copy(
            src_ref=u_v.at[h, part], dst_ref=out_hbm.at[place(hi, h)],
            send_sem=ys_sem.at[h, off], recv_sem=yr_sem.at[h, hi],
            device_id={"head": to}, device_id_type=MESH)

    def yrecv(h, j):
        return pltpu.make_async_remote_copy(
            src_ref=u_v.at[h, pl.ds(0, rows)], dst_ref=out_hbm.at[place(j, h)],
            send_sem=ys_sem.at[h, 0], recv_sem=yr_sem.at[h, j],
            device_id={"head": j}, device_id_type=MESH)

    def owncopy(h):
        part = pl.ds(pl.multiple_of(hi * rows, rows), rows)
        return pltpu.make_async_copy(u_v.at[h, part], out_hbm.at[place(hi, h)], own_sem.at[h])

    def scopy(off):
        to = hpeer(off)
        return pltpu.make_async_remote_copy(
            src_ref=rows_own.at[to], dst_ref=rows_in.at[hi], send_sem=ss_sem.at[off], recv_sem=sr_sem.at[hi],
            device_id={"head": to}, device_id_type=MESH)

    def srecv(j):
        return pltpu.make_async_remote_copy(
            src_ref=rows_own.at[j], dst_ref=rows_in.at[j], send_sem=ss_sem.at[0], recv_sem=sr_sem.at[j],
            device_id={"head": j}, device_id_type=MESH)

    def states(h):
        load(h, 0).wait()
        load(h, 1).wait()
        state = None
        for s in range(subs):
            span = slice(s * SUB, (s + 1) * SUB)
            row = clt[pl.ds(h, 1), span]
            col = jnp.transpose(jnp.broadcast_to(row, (HD, SUB)))
            clc[h, span, :] = col
            end = dlast[s, pl.ds(h, 1), :]
            keyed = (k_v[span, cols(h)].astype(f32) * jnp.exp(end - col)).astype(bf16)
            new = dot(keyed, v_v[span, cols(h)], ((0,), (0,)))
            sst[h, s] = new
            state = new if state is None else jnp.exp(end) * state + new
        mine[h] = state.astype(bf16)

    def share(h):
        for off in range(1, group):
            gcopy(h, off).start()

    def arrive(h):
        for slot in range(group):
            @pl.when(slot != r)
            def _():
                grecv(h, slot).wait_recv()

    def combine(h):
        arrive(h)
        own = mine[h].astype(f32)
        state = jnp.zeros((HD, HD), f32)
        within = state
        drop = jnp.zeros((1, HD), f32)
        before = drop
        for slot in range(group):
            here = slot == r
            within = jnp.where(here, state, within)
            before = jnp.where(here, drop, before)
            tot = jnp.where(here, tsend[pl.ds(h, 1), :], tgath[slot, pl.ds(h, 1), :])
            part = jnp.where(here, own, gath[slot, h].astype(f32))
            state = jnp.exp(tot) * state + part
            drop = drop + tot

        @pl.when(jnp.logical_not(first))
        def _():
            pltpu.make_async_remote_copy(
                src_ref=eout.at[h], dst_ref=ein.at[h], send_sem=es_sem.at[h], recv_sem=er_sem.at[h],
                device_id={"ctx": ci - group}, device_id_type=MESH).wait_recv()

        enter = jnp.where(first, 0.0, ein[h].astype(f32))
        eout[h] = (jnp.exp(drop) * enter + state).astype(bf16)

        @pl.when(jnp.logical_not(last))
        def _():
            ecopy(h).start()

        return within + jnp.exp(before) * enter

    causal = (
        lax.broadcasted_iota(jnp.int32, (SUB, SUB), 0) >= lax.broadcasted_iota(jnp.int32, (SUB, SUB), 1)
    )

    def diagonal(h, s):
        span = slice(s * SUB, (s + 1) * SUB)
        wide = jnp.concatenate([clc[h, span, :]] * (SUB // HD), axis=1)
        spread = jnp.where(causal, wide - clt[pl.ds(h, 1), span], -1e30)
        scores = dot(q_v[span, cols(h)], k_v[span, cols(h)], ((1,), (1,)))
        weights = (scores * jnp.exp(spread)).astype(bf16)
        return dot(weights, v_v[span, cols(h)], ((1,), (0,)))

    def attend(h, state, ready):
        if not ready:
            load(h, 2).wait()
        load(h, 3).wait()
        for s in range(subs):
            span = slice(s * SUB, (s + 1) * SUB)
            inner = inn[span, :] if ready else diagonal(h, s)
            across = dot(q_v[span, cols(h)], state.astype(bf16), ((1,), (0,)))
            shade = (inner + jnp.exp(clc[h, span, :]) * across).astype(bf16).astype(f32)
            acc[span, :] += shade * shade
            gate = g_v[span, cols(h)].astype(f32)
            opened = 0.5 * jnp.tanh(0.5 * gate) + 0.5
            u_v[h, span, :] = (shade * opened).astype(bf16)
            if s < subs - 1:
                state = jnp.exp(dlast[s, pl.ds(h, 1), :]) * state + sst[h, s]

    states(0)
    waits = (group - 1) + (n_head - 1) + jnp.where(first, 0, 1) + jnp.where(last, 0, 1)
    pl.semaphore_wait(barrier, waits)
    for off in range(1, group):
        tcopy(off).start()
    share(0)

    for h in range(1, ahead):
        states(h)
        share(h)
    load(0, 2).wait()
    for s in range(subs):
        inn[s * SUB:(s + 1) * SUB, :] = diagonal(0, s)
    for slot in range(group):
        @pl.when(slot != r)
        def _():
            trecv(slot).wait_recv()

    def emit(h, ready=False):
        state = combine(h)
        attend(h, state, ready)
        for off in range(1, n_head):
            ycopy(h, off).start()
        owncopy(h).start()

    def step(h, _):
        for which in range(4):
            load(h + fetch, which).start()
        emit(h)
        states(h + ahead)
        share(h + ahead)
        return 0

    def later(h, _):
        emit(h)
        states(h + ahead)
        share(h + ahead)
        return 0

    def rest(h, _):
        emit(h)
        return 0

    emit(0, True)
    if heads > fetch:
        for which in range(4):
            load(fetch, which).start()
    if heads > ahead:
        states(ahead)
        share(ahead)
    lax.fori_loop(1, heads - fetch, step, 0)
    lax.fori_loop(max(heads - fetch, 1), heads - ahead, later, 0)
    lax.fori_loop(max(heads - ahead, 1), heads, rest, 0)

    ones = jnp.ones((8, HD), f32)
    for j in range(n_head):
        rows_own[j] = dot(ones, acc[j * rows:(j + 1) * rows, :], ((1,), (1,)), lax.Precision.HIGHEST)
    for off in range(1, n_head):
        scopy(off).start()

    def finish(h, _):
        for off in range(1, group):
            gcopy(h, off).wait_send()

        @pl.when(jnp.logical_not(last))
        def _():
            ecopy(h).wait_send()

        for off in range(1, n_head):
            ycopy(h, off).wait_send()
        owncopy(h).wait()
        for j in range(n_head):
            @pl.when(j != hi)
            def _():
                yrecv(h, j).wait_recv()
        return 0

    lax.fori_loop(0, heads, finish, 0)
    for off in range(1, group):
        tcopy(off).wait_send()
    for off in range(1, n_head):
        scopy(off).wait_send()
    for j in range(n_head):
        @pl.when(j != hi)
        def _():
            srecv(j).wait_recv()
    total = rows_own[hi]
    for j in range(n_head):
        total = total + jnp.where(j == hi, 0.0, rows_in[j])
    row = lax.rsqrt(total[0:1, :] / columns + eps_norm)
    scale_ref[...] = jnp.transpose(jnp.broadcast_to(row, (HD, rows)))


def rescale(u_ref, scale_ref, gain_ref, o_ref):
    block = o_ref.shape[0]
    part = pl.ds(pl.multiple_of(pl.program_id(0) * block, block), block)
    scale = scale_ref[part, :]
    for h in range(u_ref.shape[0]):
        o_ref[:, h * HD:(h + 1) * HD] = (u_ref[h, part, :].astype(f32) * scale * gain_ref[h:h + 1, :]).astype(bf16)


def body(n_ctx, n_head, queries, keys, values, log_decay, gate, norm_gain):
    count, heads = log_decay.shape
    width = queries.shape[1]
    columns = width * n_head
    rows = count // n_head
    group = 4 if n_ctx % 4 == 0 else 1
    subs = count // SUB
    gain = norm_gain.reshape(n_head * heads, HD)
    dma = pltpu.SemaphoreType.DMA
    whole = lambda dtype: pltpu.VMEM((count, width), dtype)
    anywhere = pl.BlockSpec(memory_space=pl.ANY)
    vmem = pl.BlockSpec(memory_space=pltpu.VMEM)
    out, scale = pl.pallas_call(
        functools.partial(kernel, n_ctx, n_head, group, heads, min(2, heads), min(3, heads)),
        out_shape=(
            jax.ShapeDtypeStruct((n_head * heads, rows, HD), bf16),
            jax.ShapeDtypeStruct((rows, HD), f32),
        ),
        in_specs=[anywhere] * 4 + [vmem],
        out_specs=(anywhere, vmem),
        scratch_shapes=[
            pltpu.VMEM((count, HD), f32),
            whole(bf16), whole(bf16), whole(bf16), whole(bf16),
            pltpu.VMEM((heads, count, HD), bf16),
            pltpu.VMEM((heads, count), f32),
            pltpu.VMEM((heads, count, HD), f32),
            pltpu.VMEM((subs, heads, HD), f32),
            pltpu.VMEM((heads, subs, HD, HD), f32),
            pltpu.VMEM((heads, HD, HD), bf16),
            pltpu.VMEM((group, heads, HD, HD), bf16),
            pltpu.VMEM((heads, HD), f32),
            pltpu.VMEM((group, heads, HD), f32),
            pltpu.VMEM((heads, HD, HD), bf16),
            pltpu.VMEM((heads, HD, HD), bf16),
            pltpu.VMEM((count, HD), f32),
            pltpu.VMEM((n_head, 8, rows), f32),
            pltpu.VMEM((n_head, 8, rows), f32),
            dma((4, heads)),
            dma((heads, group)), dma((heads, group)),
            dma((group,)), dma((group,)),
            dma((heads,)), dma((heads,)),
            dma((heads, n_head)), dma((heads, n_head)),
            dma((heads,)),
            dma((n_head,)), dma((n_head,)),
        ],
        compiler_params=pltpu.CompilerParams(
            collective_id=0, has_side_effects=True, vmem_limit_bytes=46 * 1024 * 1024
        ),
        cost_estimate=pl.CostEstimate(
            flops=heads * count * HD * (4 * SUB + 4 * HD),
            bytes_accessed=5 * count * width * 2,
            transcendentals=heads * count * (SUB + 3 * HD),
        ),
    )(queries, keys, values, gate, log_decay.T)
    block = min(64, rows)
    return pl.pallas_call(
        rescale,
        grid=(rows // block,),
        out_shape=jax.ShapeDtypeStruct((rows, columns), bf16),
        in_specs=[vmem, vmem, vmem],
        out_specs=pl.BlockSpec((block, columns), lambda i: (i, 0)),
        compiler_params=pltpu.CompilerParams(vmem_limit_bytes=16 * 1024 * 1024),
        cost_estimate=pl.CostEstimate(
            flops=rows * columns, bytes_accessed=4 * rows * columns, transcendentals=rows),
    )(out, scale, gain)


def solution(mesh):
    spec = P("ctx", "head")
    return jax.shard_map(
        functools.partial(body, mesh.shape["ctx"], mesh.shape["head"]),
        mesh=mesh,
        in_specs=(spec, spec, spec, spec, spec, P()),
        out_specs=P(("ctx", "head"), None),
        check_vma=False,
    )
```

```python
import functools

import jax
import jax.numpy as jnp
from jax import lax
from jax.experimental import pallas as pl
from jax.experimental.pallas import tpu as pltpu
from jax.sharding import PartitionSpec as P

eps_norm = 1e-05
HD = 128
SUB = 256
f32 = jnp.float32
bf16 = jnp.bfloat16
MESH = pl.DeviceIdType.MESH


def dot(a, b, dims, precision=None):
    return lax.dot_general(a, b, (dims, ((), ())), precision=precision, preferred_element_type=f32)


def kernel(
    n_ctx, n_head, group, heads, ahead, fetch,
    q_hbm, k_hbm, v_hbm, g_hbm, ld_ref,
    out_hbm, scale_ref,
    inn, q_v, k_v, v_v, g_v, u_v, clt, clc, dlast, sst, mine, gath, tsend, tgath, ein, eout, acc, rows_own, rows_in,
    load_sem, gs_sem, gr_sem, ts_sem, tr_sem, es_sem, er_sem, ys_sem, yr_sem, own_sem, ss_sem, sr_sem,
):
    count = ld_ref.shape[1]
    columns = n_head * heads * HD
    subs = count // SUB
    rows = count // n_head
    planes = n_ctx // group
    ci = lax.axis_index("ctx")
    hi = lax.axis_index("head")
    plane = ci // group
    r = lax.rem(ci, group)
    base = plane * group
    first = plane == 0
    last = plane == planes - 1

    def peer(off):
        return base + lax.rem(r + off, group)

    def hpeer(off):
        return lax.rem(hi + off, n_head)

    barrier = pltpu.get_barrier_semaphore()

    def greet(**where):
        pl.semaphore_signal(barrier, inc=1, device_id=where, device_id_type=MESH)

    for off in range(1, group):
        greet(ctx=peer(off))
    for off in range(1, n_head):
        greet(head=hpeer(off))

    @pl.when(jnp.logical_not(first))
    def _():
        greet(ctx=ci - group)

    @pl.when(jnp.logical_not(last))
    def _():
        greet(ctx=ci + group)

    def cols(h):
        return pl.ds(pl.multiple_of(h * HD, HD), HD)

    def load(h, which):
        src, dst = ((k_hbm, k_v), (v_hbm, v_v), (q_hbm, q_v), (g_hbm, g_v))[which]
        return pltpu.make_async_copy(src.at[:, cols(h)], dst.at[:, cols(h)], load_sem.at[which, h])

    for h in range(fetch):
        for which in range(4):
            load(h, which).start()
    acc[...] = jnp.zeros_like(acc)

    up = (
        lax.broadcasted_iota(jnp.int32, (SUB, SUB), 0) <= lax.broadcasted_iota(jnp.int32, (SUB, SUB), 1)
    ).astype(f32).astype(bf16)
    parts = []
    for s in range(subs):
        left = ld_ref[:, s * SUB:(s + 1) * SUB]
        for _ in range(3):
            part = left.astype(bf16).astype(f32)
            parts.append(part)
            left = left - part
    sums = dot(jnp.concatenate(parts, axis=0).astype(bf16), up, ((1,), (0,)))
    total = jnp.zeros((heads, 1), f32)
    for s in range(subs):
        at = 3 * s * heads
        cl = (sums[at + 2 * heads:at + 3 * heads] + sums[at + heads:at + 2 * heads]) + sums[at:at + heads]
        clt[:, s * SUB:(s + 1) * SUB] = cl
        end = cl[:, SUB - 1:SUB]
        dlast[s] = jnp.broadcast_to(end, (heads, HD))
        total = total + end
    tsend[...] = jnp.broadcast_to(total, (heads, HD))

    def tcopy(off):
        return pltpu.make_async_remote_copy(
            src_ref=tsend, dst_ref=tgath.at[r], send_sem=ts_sem.at[off], recv_sem=tr_sem.at[r],
            device_id={"ctx": peer(off)}, device_id_type=MESH)

    def gcopy(h, off):
        return pltpu.make_async_remote_copy(
            src_ref=mine.at[h], dst_ref=gath.at[r, h], send_sem=gs_sem.at[h, off], recv_sem=gr_sem.at[h, r],
            device_id={"ctx": peer(off)}, device_id_type=MESH)

    def grecv(h, slot):
        return pltpu.make_async_remote_copy(
            src_ref=mine.at[h], dst_ref=gath.at[slot, h], send_sem=gs_sem.at[h, 0], recv_sem=gr_sem.at[h, slot],
            device_id={"ctx": slot + base}, device_id_type=MESH)

    def trecv(slot):
        return pltpu.make_async_remote_copy(
            src_ref=tsend, dst_ref=tgath.at[slot], send_sem=ts_sem.at[0], recv_sem=tr_sem.at[slot],
            device_id={"ctx": slot + base}, device_id_type=MESH)

    def ecopy(h):
        return pltpu.make_async_remote_copy(
            src_ref=eout.at[h], dst_ref=ein.at[h], send_sem=es_sem.at[h], recv_sem=er_sem.at[h],
            device_id={"ctx": ci + group}, device_id_type=MESH)

    def place(j, h):
        return j * heads + h

    def ycopy(h, off):
        to = hpeer(off)
        part = pl.ds(pl.multiple_of(to * rows, rows), rows)
        return pltpu.make_async_remote_copy(
            src_ref=u_v.at[h, part], dst_ref=out_hbm.at[place(hi, h)],
            send_sem=ys_sem.at[h, off], recv_sem=yr_sem.at[h, hi],
            device_id={"head": to}, device_id_type=MESH)

    def yrecv(h, j):
        return pltpu.make_async_remote_copy(
            src_ref=u_v.at[h, pl.ds(0, rows)], dst_ref=out_hbm.at[place(j, h)],
            send_sem=ys_sem.at[h, 0], recv_sem=yr_sem.at[h, j],
            device_id={"head": j}, device_id_type=MESH)

    def owncopy(h):
        part = pl.ds(pl.multiple_of(hi * rows, rows), rows)
        return pltpu.make_async_copy(u_v.at[h, part], out_hbm.at[place(hi, h)], own_sem.at[h])

    def scopy(off):
        to = hpeer(off)
        return pltpu.make_async_remote_copy(
            src_ref=rows_own.at[to], dst_ref=rows_in.at[hi], send_sem=ss_sem.at[off], recv_sem=sr_sem.at[hi],
            device_id={"head": to}, device_id_type=MESH)

    def srecv(j):
        return pltpu.make_async_remote_copy(
            src_ref=rows_own.at[j], dst_ref=rows_in.at[j], send_sem=ss_sem.at[0], recv_sem=sr_sem.at[j],
            device_id={"head": j}, device_id_type=MESH)

    def states(h):
        load(h, 0).wait()
        load(h, 1).wait()
        state = None
        for s in range(subs):
            span = slice(s * SUB, (s + 1) * SUB)
            row = clt[pl.ds(h, 1), span]
            col = jnp.transpose(jnp.broadcast_to(row, (HD, SUB)))
            clc[h, span, :] = col
            end = dlast[s, pl.ds(h, 1), :]
            keyed = (k_v[span, cols(h)].astype(f32) * jnp.exp(end - col)).astype(bf16)
            new = dot(keyed, v_v[span, cols(h)], ((0,), (0,)))
            sst[h, s] = new
            state = new if state is None else jnp.exp(end) * state + new
        mine[h] = state.astype(bf16)

    def share(h):
        for off in range(1, group):
            gcopy(h, off).start()

    def arrive(h):
        for slot in range(group):
            @pl.when(slot != r)
            def _():
                grecv(h, slot).wait_recv()

    def combine(h):
        arrive(h)
        own = mine[h].astype(f32)
        state = jnp.zeros((HD, HD), f32)
        within = state
        drop = jnp.zeros((1, HD), f32)
        before = drop
        for slot in range(group):
            here = slot == r
            within = jnp.where(here, state, within)
            before = jnp.where(here, drop, before)
            tot = jnp.where(here, tsend[pl.ds(h, 1), :], tgath[slot, pl.ds(h, 1), :])
            part = jnp.where(here, own, gath[slot, h].astype(f32))
            state = jnp.exp(tot) * state + part
            drop = drop + tot

        @pl.when(jnp.logical_not(first))
        def _():
            pltpu.make_async_remote_copy(
                src_ref=eout.at[h], dst_ref=ein.at[h], send_sem=es_sem.at[h], recv_sem=er_sem.at[h],
                device_id={"ctx": ci - group}, device_id_type=MESH).wait_recv()

        enter = jnp.where(first, 0.0, ein[h].astype(f32))
        eout[h] = (jnp.exp(drop) * enter + state).astype(bf16)

        @pl.when(jnp.logical_not(last))
        def _():
            ecopy(h).start()

        return within + jnp.exp(before) * enter

    causal = (
        lax.broadcasted_iota(jnp.int32, (SUB, SUB), 0) >= lax.broadcasted_iota(jnp.int32, (SUB, SUB), 1)
    )

    def diagonal(h, s):
        span = slice(s * SUB, (s + 1) * SUB)
        wide = jnp.concatenate([clc[h, span, :]] * (SUB // HD), axis=1)
        spread = jnp.where(causal, wide - clt[pl.ds(h, 1), span], -1e30)
        scores = dot(q_v[span, cols(h)], k_v[span, cols(h)], ((1,), (1,)))
        weights = (scores * jnp.exp(spread)).astype(bf16)
        return dot(weights, v_v[span, cols(h)], ((1,), (0,)))

    def attend(h, state, ready):
        if not ready:
            load(h, 2).wait()
        load(h, 3).wait()
        for s in range(subs):
            span = slice(s * SUB, (s + 1) * SUB)
            inner = inn[span, :] if ready else diagonal(h, s)
            across = dot(q_v[span, cols(h)], state.astype(bf16), ((1,), (0,)))
            shade = (inner + jnp.exp(clc[h, span, :]) * across).astype(bf16).astype(f32)
            acc[span, :] += shade * shade
            gate = g_v[span, cols(h)].astype(f32)
            opened = 0.5 * jnp.tanh(0.5 * gate) + 0.5
            u_v[h, span, :] = (shade * opened).astype(bf16)
            if s < subs - 1:
                state = jnp.exp(dlast[s, pl.ds(h, 1), :]) * state + sst[h, s]

    states(0)
    waits = (group - 1) + (n_head - 1) + jnp.where(first, 0, 1) + jnp.where(last, 0, 1)
    pl.semaphore_wait(barrier, waits)
    for off in range(1, group):
        tcopy(off).start()
    share(0)

    for h in range(1, ahead):
        states(h)
        share(h)
    load(0, 2).wait()
    for s in range(subs):
        inn[s * SUB:(s + 1) * SUB, :] = diagonal(0, s)
    for slot in range(group):
        @pl.when(slot != r)
        def _():
            trecv(slot).wait_recv()

    def emit(h, ready=False):
        state = combine(h)
        attend(h, state, ready)
        for off in range(1, n_head):
            ycopy(h, off).start()
        owncopy(h).start()

    def step(h, _):
        for which in range(4):
            load(h + fetch, which).start()
        emit(h)
        states(h + ahead)
        share(h + ahead)
        return 0

    def later(h, _):
        emit(h)
        states(h + ahead)
        share(h + ahead)
        return 0

    def rest(h, _):
        emit(h)
        return 0

    emit(0, True)
    if heads > fetch:
        for which in range(4):
            load(fetch, which).start()
    if heads > ahead:
        states(ahead)
        share(ahead)
    lax.fori_loop(1, heads - fetch, step, 0)
    lax.fori_loop(max(heads - fetch, 1), heads - ahead, later, 0)
    lax.fori_loop(max(heads - ahead, 1), heads, rest, 0)

    ones = jnp.ones((8, HD), f32)
    for j in range(n_head):
        rows_own[j] = dot(ones, acc[j * rows:(j + 1) * rows, :], ((1,), (1,)), lax.Precision.HIGHEST)
    for off in range(1, n_head):
        scopy(off).start()

    def finish(h, _):
        for off in range(1, group):
            gcopy(h, off).wait_send()

        @pl.when(jnp.logical_not(last))
        def _():
            ecopy(h).wait_send()

        for off in range(1, n_head):
            ycopy(h, off).wait_send()
        owncopy(h).wait()
        for j in range(n_head):
            @pl.when(j != hi)
            def _():
                yrecv(h, j).wait_recv()
        return 0

    lax.fori_loop(0, heads, finish, 0)
    for off in range(1, group):
        tcopy(off).wait_send()
    for off in range(1, n_head):
        scopy(off).wait_send()
    for j in range(n_head):
        @pl.when(j != hi)
        def _():
            srecv(j).wait_recv()
    total = rows_own[hi]
    for j in range(n_head):
        total = total + jnp.where(j == hi, 0.0, rows_in[j])
    row = lax.rsqrt(total[0:1, :] / columns + eps_norm)
    scale_ref[...] = jnp.transpose(jnp.broadcast_to(row, (HD, rows)))


def rescale(u_ref, scale_ref, gain_ref, o_ref):
    scale = scale_ref[...]
    for h in range(u_ref.shape[0]):
        o_ref[:, h * HD:(h + 1) * HD] = (u_ref[h].astype(f32) * scale * gain_ref[h:h + 1, :]).astype(bf16)


def body(n_ctx, n_head, queries, keys, values, log_decay, gate, norm_gain):
    count, heads = log_decay.shape
    width = queries.shape[1]
    columns = width * n_head
    rows = count // n_head
    group = 4 if n_ctx % 4 == 0 else 1
    subs = count // SUB
    gain = norm_gain.reshape(n_head * heads, HD)
    dma = pltpu.SemaphoreType.DMA
    whole = lambda dtype: pltpu.VMEM((count, width), dtype)
    anywhere = pl.BlockSpec(memory_space=pl.ANY)
    vmem = pl.BlockSpec(memory_space=pltpu.VMEM)
    out, scale = pl.pallas_call(
        functools.partial(kernel, n_ctx, n_head, group, heads, min(2, heads), min(3, heads)),
        out_shape=(
            jax.ShapeDtypeStruct((n_head * heads, rows, HD), bf16),
            jax.ShapeDtypeStruct((rows, HD), f32),
        ),
        in_specs=[anywhere] * 4 + [vmem],
        out_specs=(anywhere, vmem),
        scratch_shapes=[
            pltpu.VMEM((count, HD), f32),
            whole(bf16), whole(bf16), whole(bf16), whole(bf16),
            pltpu.VMEM((heads, count, HD), bf16),
            pltpu.VMEM((heads, count), f32),
            pltpu.VMEM((heads, count, HD), f32),
            pltpu.VMEM((subs, heads, HD), f32),
            pltpu.VMEM((heads, subs, HD, HD), f32),
            pltpu.VMEM((heads, HD, HD), bf16),
            pltpu.VMEM((group, heads, HD, HD), bf16),
            pltpu.VMEM((heads, HD), f32),
            pltpu.VMEM((group, heads, HD), f32),
            pltpu.VMEM((heads, HD, HD), bf16),
            pltpu.VMEM((heads, HD, HD), bf16),
            pltpu.VMEM((count, HD), f32),
            pltpu.VMEM((n_head, 8, rows), f32),
            pltpu.VMEM((n_head, 8, rows), f32),
            dma((4, heads)),
            dma((heads, group)), dma((heads, group)),
            dma((group,)), dma((group,)),
            dma((heads,)), dma((heads,)),
            dma((heads, n_head)), dma((heads, n_head)),
            dma((heads,)),
            dma((n_head,)), dma((n_head,)),
        ],
        compiler_params=pltpu.CompilerParams(
            collective_id=0, has_side_effects=True, vmem_limit_bytes=46 * 1024 * 1024
        ),
        cost_estimate=pl.CostEstimate(
            flops=heads * count * HD * (4 * SUB + 4 * HD),
            bytes_accessed=5 * count * width * 2,
            transcendentals=heads * count * (SUB + 3 * HD),
        ),
    )(queries, keys, values, gate, log_decay.T)
    block = min(128, rows)
    return pl.pallas_call(
        rescale,
        grid=(rows // block,),
        out_shape=jax.ShapeDtypeStruct((rows, columns), bf16),
        in_specs=[
            pl.BlockSpec((n_head * heads, block, HD), lambda i: (0, i, 0)),
            pl.BlockSpec((block, HD), lambda i: (i, 0)),
            vmem,
        ],
        out_specs=pl.BlockSpec((block, columns), lambda i: (i, 0)),
        compiler_params=pltpu.CompilerParams(vmem_limit_bytes=16 * 1024 * 1024),
        cost_estimate=pl.CostEstimate(
            flops=rows * columns, bytes_accessed=4 * rows * columns, transcendentals=rows),
    )(out, scale, gain)


def solution(mesh):
    spec = P("ctx", "head")
    return jax.shard_map(
        functools.partial(body, mesh.shape["ctx"], mesh.shape["head"]),
        mesh=mesh,
        in_specs=(spec, spec, spec, spec, spec, P()),
        out_specs=P(("ctx", "head"), None),
        check_vma=False,
    )
```
